128 devices in a mesh: ctx: 8 (over x, core), ch: 16 (over y, z).
Axes of the slice: x: 4, y: 4, z: 4, core: 2. Of those that a mesh axis runs over, the one named last changes fastest.
Arguments:
- query_branch: bfloat16 [8192, 8192], P('ctx', 'ch'), may hold values from -6 to 6
- key_branch: bfloat16 [8192, 8192], P('ctx', 'ch'), may hold values from -6 to 6
- value_branch: bfloat16 [8192, 8192], P('ctx', 'ch'), may hold values from -6 to 6
- residue: float32 [16, 8192], P(None, 'ch'), may hold values from -0.15 to 0.15
- decay_rate: float32 [16, 8192], P(None, 'ch'), may hold values from 6.1035156e-05 to 0.04
- skip_gain: float32 [8192], P('ch'), may hold values from 0.5 to 1.5
- out_weight: bfloat16 [8192, 8192], P('ch'), may hold values from -0.0625 to 0.0625
Outputs:
- layer_output: bfloat16 [8192, 8192], P('ctx', 'ch')
The draws below stay inside these ranges and needn't reach their ends.
All inputs are finite; a program needn't handle non-finite values.
Results may differ from the reference program's by a relative error of at most 0.018.
Values may be sent and summed in bfloat16 or wider, within the bound.
A program may use at most 128 MiB of HBM per device.

```python
import math
import jax
import jax.numpy as jnp
from jax import lax

D = 8192
M = 16
SEQ = 8192
N_CH = 16


def block_scale(own_key, shape, pieces, least, top_value):
    factor_of = 1.0
    for axis_at, blocks in pieces:
        steps = jax.random.uniform(jax.random.fold_in(jax.random.fold_in(own_key, 6), axis_at), (blocks,), jnp.float32, least / len(pieces), top_value / len(pieces))
        factor_of = factor_of * jnp.repeat(jnp.exp(steps), shape[axis_at] // blocks).reshape((-1,) + (1,) * (len(shape) - 1 - axis_at))
    return factor_of


def bell_draw(key, dims, deviation, most, pieces=(), kind=jnp.bfloat16):
    loudness = block_scale(key, dims, pieces, -0.22, 0.18) if pieces else 1.0
    array = jax.random.normal(key, dims, jnp.float32) * deviation * loudness
    return jnp.minimum(jnp.maximum(array, -most), most).astype(kind)


def setup_inputs(seed: int = 0) -> dict:
    key_list = jax.random.split(jax.random.key(seed), 8)
    query_branch = bell_draw(key_list[0], (SEQ, D), 1.0, 6.0, ((0, 8), (1, 16)))
    key_branch = bell_draw(key_list[1], (SEQ, D), 1.0, 6.0, ((0, 8), (1, 16)))
    value_branch = bell_draw(key_list[2], (SEQ, D), 1.0, 6.0, ((0, 8), (1, 16)))
    residue = bell_draw(key_list[3], (M, D), 0.03, 0.15, ((1, 16),), jnp.float32)
    decay_rate = jnp.clip(jnp.exp(math.log(0.04) - 6.4851847 * jax.random.uniform(key_list[4], (M, D), jnp.float32) ** block_scale(key_list[4], (M, D), ((1, 16),), -0.2, 0.2)), 6.103515625e-05, 0.04)
    skip_gain = jnp.clip(0.5 + 1.0 * jax.random.uniform(key_list[5], (D,), jnp.float32) ** block_scale(key_list[5], (D,), ((0, 16),), -0.2, 0.2), 0.5, 1.5)
    out_weight = bell_draw(key_list[6], (D, D), D ** -0.5, 0.0625, ((0, 16),))
    return dict(query_branch=query_branch, key_branch=key_branch, value_branch=value_branch, residue=residue, decay_rate=decay_rate, skip_gain=skip_gain, out_weight=out_weight)


def reference(query_branch, key_branch, value_branch, residue, decay_rate, skip_gain, out_weight):
    gated = (key_branch.astype(jnp.float32) * value_branch.astype(jnp.float32)).astype(jnp.bfloat16)
    signal = gated.astype(jnp.float32)
    width = math.gcd(D, 256)
    groups = D // width
    lag_steps = jnp.arange(SEQ, dtype=jnp.float32)
    fft_length = 2 * SEQ

    def convolve(operands):
        res_block, rate_block, sig_block = operands
        kernel = jnp.zeros((SEQ, width), jnp.float32)
        for mode in range(M):
            kernel = kernel + res_block[mode][None, :] * jnp.exp(-rate_block[mode][None, :] * lag_steps[:, None])
        spectrum = jnp.fft.rfft(kernel, n=fft_length, axis=0) * jnp.fft.rfft(sig_block, n=fft_length, axis=0)
        return jnp.fft.irfft(spectrum, n=fft_length, axis=0)[:SEQ]

    res_groups = residue.reshape(M, groups, width).transpose(1, 0, 2)
    rate_groups = decay_rate.reshape(M, groups, width).transpose(1, 0, 2)
    sig_groups = signal.reshape(SEQ, groups, width).transpose(1, 0, 2)
    convolved = lax.map(convolve, (res_groups, rate_groups, sig_groups))
    convolved = convolved.transpose(1, 0, 2).reshape(SEQ, D)
    mixed = convolved + skip_gain[None, :] * signal
    gated_out = (query_branch.astype(jnp.float32) * mixed).astype(jnp.bfloat16)
    shard_width = D // N_CH

    def add_share(total, index):
        start = (index * shard_width).astype(jnp.int32)
        rows_in = lax.dynamic_slice_in_dim(gated_out, start, shard_width, 1)
        rows_weight = lax.dynamic_slice_in_dim(out_weight, start, shard_width, 0)
        share = jnp.dot(rows_in, rows_weight, preferred_element_type=jnp.float32).astype(jnp.bfloat16)
        return total + share.astype(jnp.float32), None

    total, unused = lax.scan(add_share, jnp.zeros((SEQ, D), jnp.float32), jnp.arange(N_CH, dtype=jnp.int32))
    return total.astype(jnp.bfloat16)
```

```python
import functools

import jax
import jax.numpy as jnp
from jax import lax
from jax.experimental import pallas as pl
from jax.experimental.pallas import tpu as pltpu
from jax.sharding import PartitionSpec as P

MESH = pl.DeviceIdType.MESH
SEGS = 8
CHUNKS = 8
RING = 4
LANES = 128


def kernel(
    q_ref, k_ref, v_ref, res_ref, rate_ref, skip_ref, w_ref, out_ref,
    gat, st, ends, mixed, wblk, gbuf, s2, r2, s1, r1,
    lw_sem, y_s, y_r, x_s, x_r, c_s, c_r, e_s, e_r, g_s, g_r, z_s, z_r,
):
    tok, chan = k_ref.shape
    poles = res_ref.shape[0]
    seg_len = tok // SEGS
    steps = seg_len // CHUNKS
    rows = SEGS * steps
    half = rows // 2
    groups = chan // LANES
    n_ctx = 2 * RING
    slice_rows = chan // n_ctx

    ctx = lax.axis_index("ctx")
    ch = lax.axis_index("ch")
    x, core = ctx // 2, ctx % 2
    y, z = ch // RING, ch % RING

    def up(a, by):
        return lax.rem(a + by + RING, RING)

    def on_x(by):
        return (up(x, by) * 2 + core, ch)

    def on_y(by):
        return (ctx, up(y, by) * RING + z)

    def on_z(by):
        return (ctx, y * RING + up(z, by))

    partner = (x * 2 + 1 - core, ch)

    def remote(src, dst, send, recv, device):
        return pltpu.make_async_remote_copy(
            src_ref=src, dst_ref=dst, send_sem=send, recv_sem=recv, device_id=device, device_id_type=MESH
        )

    def z_of(b):
        return (2, 1, -1, 0)[b]

    def w_cols(y_at, b):
        start = (y_at * RING + up(z, z_of(b))) * chan
        return pl.ds(pl.multiple_of(start, chan), chan)

    def local_w(b, s):
        return pltpu.make_async_copy(
            w_ref.at[pl.ds(s * slice_rows, slice_rows), w_cols(y, b)],
            wblk.at[b, 0, s // 2, s % 2],
            lw_sem.at[b, s],
        )

    def y_copy(b, j):
        return remote(
            w_ref.at[pl.ds(pl.multiple_of(ctx * slice_rows, slice_rows), slice_rows), w_cols(up(y, -j), b)],
            wblk.at[b, j, x, core],
            y_s.at[b, j - 1],
            y_r.at[b, j - 1],
            on_y(-j),
        )

    def x_copy(b, kind):
        if kind < 2:
            ref = wblk.at[b, pl.ds(1, RING - 1), x, core]
        elif kind == 2:
            ref = wblk.at[b, pl.ds(1, RING - 1), up(x, -1), core, pl.ds(0, slice_rows // 2)]
        else:
            ref = wblk.at[b, pl.ds(1, RING - 1), up(x, 1), core, pl.ds(slice_rows // 2, slice_rows // 2)]
        return remote(ref, ref, x_s.at[b, kind], x_r.at[b, kind], on_x(1 if kind % 2 == 0 else -1))

    def c_copy(b):
        ref = wblk.at[b, pl.ds(1, RING - 1), :, core]
        return remote(ref, ref, c_s.at[b], c_r.at[b], partner)

    def e_copy(o):
        ref = ends.at[ctx]
        return remote(ref, ref, e_s.at[o - 1], e_r.at[o - 1], (lax.rem(ctx + o, n_ctx), ch))

    def g_copy(c, kind):
        if kind < 2:
            src = gbuf.at[c, 0]
            dst = gbuf.at[c, 3 if kind == 0 else 1]
        elif kind == 2:
            src = gbuf.at[c, 3, pl.ds(0, half)]
            dst = gbuf.at[c, 2, pl.ds(0, half)]
        else:
            src = gbuf.at[c, 1, pl.ds(half, half)]
            dst = gbuf.at[c, 2, pl.ds(half, half)]
        return remote(src, dst, g_s.at[c, kind], g_r.at[c, kind], on_y(1 if kind % 2 == 0 else -1))

    def z_copy(c, kind):
        if kind < 2:
            src = s2.at[c, pl.ds(kind * half, half)]
            dst = r2.at[c, pl.ds(kind * half, half)]
        else:
            src = s1.at[c, kind - 2]
            dst = r1.at[c, kind - 2]
        return remote(src, dst, z_s.at[c, kind], z_r.at[c, kind], on_z(1 if kind % 2 == 0 else -1))

    barrier = pltpu.get_barrier_semaphore()
    others = [(lax.rem(ctx + o, n_ctx), ch) for o in range(1, n_ctx)]
    others += [on_y(o) for o in range(1, RING)] + [on_z(1), on_z(-1)]
    for device in others:
        pl.semaphore_signal(barrier, inc=1, device_id=device, device_id_type=MESH)
    pl.semaphore_wait(barrier, len(others))

    for b in range(RING):
        for j in (1, 3, 2):
            y_copy(b, j).start()
    for b in range(RING):
        for s in range(n_ctx):
            local_w(b, s).start()

    @pl.loop(0, tok // 16)
    def _(i):
        at = pl.ds(pl.multiple_of(i * 16, 16), 16)
        product = k_ref[at, :].astype(jnp.float32) * v_ref[at, :].astype(jnp.float32)
        product = product.astype(jnp.bfloat16).astype(jnp.float32)
        for grp in range(groups):
            gat[grp, at, :] = product[:, grp * LANES : (grp + 1) * LANES]

    @pl.loop(0, groups)
    def _(grp):
        lanes = pl.ds(pl.multiple_of(grp * LANES, LANES), LANES)
        rate = rate_ref[:, lanes]
        decay = jnp.exp(-rate)
        d = [jnp.broadcast_to(decay[m : m + 1], (SEGS, LANES)) for m in range(poles)]

        def step(j, s):
            g = gat[grp, pl.ds(j, SEGS, stride=seg_len), :]
            return tuple(s[m] * d[m] + g for m in range(poles))

        zero = jnp.zeros((SEGS, LANES), jnp.float32)
        s = lax.fori_loop(0, seg_len, step, (zero,) * poles, unroll=4)
        seg = lax.broadcasted_iota(jnp.int32, (SEGS, LANES), 0)
        last = []
        for m in range(poles):
            run = s[m]
            for by in (1, 2, 4):
                ratio = jnp.exp(-rate[m : m + 1] * float(seg_len * by))
                run = run + jnp.where(seg >= by, pltpu.roll(run, by, 0) * ratio, 0.0)
            st[m, :, lanes] = run
            last.append(run[SEGS - 1 :])
        ends[ctx, :, lanes] = jnp.concatenate(last, axis=0)

    for o in range(1, n_ctx):
        e_copy(o).start()

    def w_y_arrived(b):
        for j in range(1, RING):
            y_copy(b, j).wait_recv()
        x_copy(b, 0).start()
        x_copy(b, 1).start()

    def w_x_arrived(b):
        x_copy(b, 0).wait_recv()
        x_copy(b, 2).start()
        x_copy(b, 1).wait_recv()
        x_copy(b, 3).start()

    def w_x_complete(b):
        x_copy(b, 2).wait_recv()
        x_copy(b, 3).wait_recv()
        c_copy(b).start()

    def w_complete(b):
        c_copy(b).wait_recv()
        for s in range(n_ctx):
            local_w(b, s).wait()

    w_y_arrived(0)
    for o in range(1, n_ctx):
        e_copy(o).wait_recv()

    @pl.loop(0, groups)
    def _(grp):
        lanes = pl.ds(pl.multiple_of(grp * LANES, LANES), LANES)
        rate = rate_ref[:, lanes]
        whole = jnp.exp(-rate * float(tok))
        state_in = jnp.zeros((poles, LANES), jnp.float32)
        for o in range(n_ctx - 1):
            state_in = jnp.where(o < ctx, state_in * whole + ends[o, :, lanes], state_in)
        seg = lax.broadcasted_iota(jnp.int32, (SEGS, LANES), 0)
        behind = seg.astype(jnp.float32) * float(seg_len)
        for m in range(poles):
            before = jnp.where(seg >= 1, pltpu.roll(st[m, :, lanes], 1, 0), 0.0)
            st[m, :, lanes] = before + jnp.exp(-rate[m : m + 1] * behind) * state_in[m : m + 1]

    def second_pass(c):
        @pl.loop(0, groups)
        def _(grp):
            lanes = pl.ds(pl.multiple_of(grp * LANES, LANES), LANES)
            decay = jnp.exp(-rate_ref[:, lanes])
            d = [jnp.broadcast_to(decay[m : m + 1], (SEGS, LANES)) for m in range(poles)]
            weight = res_ref[:, lanes]
            w = [jnp.broadcast_to(weight[m : m + 1], (SEGS, LANES)) for m in range(poles)]
            skip = jnp.broadcast_to(skip_ref[:, lanes], (SEGS, LANES))

            def step(j, s):
                g = gat[grp, pl.ds(c * steps + j, SEGS, stride=seg_len), :]
                s = tuple(s[m] * d[m] + g for m in range(poles))
                parts = [s[m] * w[m] for m in range(poles)]
                while len(parts) > 1:
                    parts = [a + b for a, b in zip(parts[::2], parts[1::2])]
                mixed[grp, pl.ds(j, SEGS, stride=steps), :] = parts[0] + skip * g
                return s

            s = lax.fori_loop(0, steps, step, tuple(st[m, :, lanes] for m in range(poles)), unroll=2)
            for m in range(poles):
                st[m, :, lanes] = s[m]

        @pl.loop(0, SEGS)
        def _(i):
            at = pl.ds(pl.multiple_of(i * steps, steps), steps)
            q = q_ref[pl.ds(pl.multiple_of(i * seg_len + c * steps, steps), steps), :]
            for grp in range(groups):
                lanes = slice(grp * LANES, (grp + 1) * LANES)
                gbuf[c, 0, at, lanes] = (q[:, lanes].astype(jnp.float32) * mixed[grp, at, :]).astype(jnp.bfloat16)

        g_copy(c, 0).start()
        g_copy(c, 1).start()

    def g_arrived(c):
        g_copy(c, 0).wait_recv()
        g_copy(c, 2).start()
        g_copy(c, 1).wait_recv()
        g_copy(c, 3).start()

    def product(c, b):
        total = None
        for j in range(RING):
            weight = wblk[b, j].reshape(chan, chan)
            part = jnp.dot(gbuf[c, j], weight, preferred_element_type=jnp.float32)
            total = part if total is None else total + part
        return total

    second_pass(0)
    w_y_arrived(1)
    w_x_arrived(0)
    second_pass(1)
    w_y_arrived(2)
    w_x_arrived(1)
    w_x_complete(0)
    second_pass(2)
    w_y_arrived(3)
    g_arrived(0)

    @pl.loop(0, CHUNKS + 4)
    def _(i):
        @pl.when(i + 3 < CHUNKS)
        def _():
            second_pass(i + 3)

        @pl.when(i + 1 < CHUNKS)
        def _():
            g_arrived(i + 1)

        @pl.when(i < 2)
        def _():
            w_x_arrived(i + 2)

        @pl.when(i < 3)
        def _():
            w_x_complete(i + 1)

        @pl.when(i == 0)
        def _():
            w_complete(0)

        @pl.when(i == 1)
        def _():
            w_complete(1)

        @pl.when(i == 2)
        def _():
            w_complete(2)

        @pl.when(i == 4)
        def _():
            w_complete(3)

        @pl.when(i < CHUNKS)
        def _():
            g_copy(i, 2).wait_recv()
            g_copy(i, 3).wait_recv()
            s2[i] = product(i, 0).astype(jnp.bfloat16)
            z_copy(i, 0).start()
            z_copy(i, 1).start()

        @pl.when(jnp.logical_and(i >= 1, i - 1 < CHUNKS))
        def _():
            c = i - 1
            total = product(c, 1)
            z_copy(c, 0).wait_recv()
            s1[c, 0, pl.ds(0, half), :] = (total[:half] + r2[c, pl.ds(0, half), :].astype(jnp.float32)).astype(jnp.bfloat16)
            s1[c, 0, pl.ds(half, half), :] = total[half:].astype(jnp.bfloat16)
            z_copy(c, 2).start()

        @pl.when(jnp.logical_and(i >= 2, i - 2 < CHUNKS))
        def _():
            c = i - 2
            total = product(c, 2)
            z_copy(c, 1).wait_recv()
            s1[c, 1, pl.ds(0, half), :] = total[:half].astype(jnp.bfloat16)
            s1[c, 1, pl.ds(half, half), :] = (total[half:] + r2[c, pl.ds(half, half), :].astype(jnp.float32)).astype(jnp.bfloat16)
            z_copy(c, 3).start()

        @pl.when(i >= 4)
        def _():
            c = i - 4
            total = product(c, 3)
            z_copy(c, 2).wait_recv()
            z_copy(c, 3).wait_recv()
            total = (total + r1[c, 0].astype(jnp.float32) + r1[c, 1].astype(jnp.float32)).astype(jnp.bfloat16)
            for seg in range(SEGS):
                at = pl.ds(pl.multiple_of(seg * seg_len + c * steps, steps), steps)
                out_ref[at, :] = total[seg * steps : (seg + 1) * steps]

    for o in range(1, n_ctx):
        e_copy(o).wait_send()
    for b in range(RING):
        for j in range(1, RING):
            y_copy(b, j).wait_send()
        for kind in range(4):
            x_copy(b, kind).wait_send()
        c_copy(b).wait_send()

    @pl.loop(0, CHUNKS)
    def _(c):
        for kind in range(4):
            g_copy(c, kind).wait_send()
            z_copy(c, kind).wait_send()


def shards(query_branch, key_branch, value_branch, residue, decay_rate, skip_gain, out_weight):
    tok, chan = key_branch.shape
    poles = residue.shape[0]
    rows = tok // CHUNKS
    n_ctx = 2 * RING
    dma = pltpu.SemaphoreType.DMA
    bf16, f32 = jnp.bfloat16, jnp.float32
    vmem = pl.BlockSpec(memory_space=pltpu.VMEM)
    return pl.pallas_call(
        kernel,
        out_shape=jax.ShapeDtypeStruct((tok, chan), bf16),
        in_specs=[vmem] * 6 + [pl.BlockSpec(memory_space=pl.ANY)],
        out_specs=vmem,
        scratch_shapes=[
            pltpu.VMEM((chan // LANES, tok, LANES), f32),
            pltpu.VMEM((poles, SEGS, chan), f32),
            pltpu.VMEM((n_ctx, poles, chan), f32),
            pltpu.VMEM((chan // LANES, rows, LANES), f32),
            pltpu.VMEM((RING, RING, RING, 2, chan // n_ctx, chan), bf16),
            pltpu.VMEM((CHUNKS, RING, rows, chan), bf16),
            pltpu.VMEM((CHUNKS, rows, chan), bf16),
            pltpu.VMEM((CHUNKS, rows, chan), bf16),
            pltpu.VMEM((CHUNKS, 2, rows, chan), bf16),
            pltpu.VMEM((CHUNKS, 2, rows, chan), bf16),
            dma((RING, n_ctx)),
            dma((RING, RING - 1)), dma((RING, RING - 1)),
            dma((RING, 4)), dma((RING, 4)),
            dma((RING,)), dma((RING,)),
            dma((n_ctx - 1,)), dma((n_ctx - 1,)),
            dma((CHUNKS, 4)), dma((CHUNKS, 4)),
            dma((CHUNKS, 4)), dma((CHUNKS, 4)),
        ],
        compiler_params=pltpu.CompilerParams(
            collective_id=0, has_side_effects=True, vmem_limit_bytes=50 * 1024 * 1024
        ),
        cost_estimate=pl.CostEstimate(
            flops=2 * tok * chan * chan * 16, bytes_accessed=12 * 1024 * 1024, transcendentals=0
        ),
    )(query_branch, key_branch, value_branch, residue, decay_rate, skip_gain.reshape(1, chan), out_weight)


def solution(mesh):
    in_specs = (
        P("ctx", "ch"),
        P("ctx", "ch"),
        P("ctx", "ch"),
        P(None, "ch"),
        P(None, "ch"),
        P("ch"),
        P("ch", None),
    )
    return jax.shard_map(shards, mesh=mesh, in_specs=in_specs, out_specs=P("ctx", "ch"), check_vma=False)
```

```python
import functools

import jax
import jax.numpy as jnp
from jax import lax
from jax.experimental import pallas as pl
from jax.experimental.pallas import tpu as pltpu
from jax.sharding import PartitionSpec as P

MESH = pl.DeviceIdType.MESH
SEGS = 8
CHUNKS = 8
RING = 4
LANES = 128


def kernel(
    q_hbm, k_hbm, v_hbm, res_hbm, rate_hbm, skip_hbm, w_ref, out_ref,
    q_ref, k_ref, v_ref, res_ref, rate_ref, skip_ref, out_buf,
    gat, st, ends, mixed, wblk, gbuf, s2, r2, s1, r1,
    in_sem, kv_sem, out_sem, lw_sem, y_s, y_r, x_s, x_r, c_s, c_r, e_s, e_r, g_s, g_r, z_s, z_r,
):
    tok, chan = k_ref.shape
    poles = res_ref.shape[0]
    seg_len = tok // SEGS
    steps = seg_len // CHUNKS
    rows = SEGS * steps
    half = rows // 2
    groups = chan // LANES
    n_ctx = 2 * RING
    slice_rows = chan // n_ctx

    ctx = lax.axis_index("ctx")
    ch = lax.axis_index("ch")
    x, core = ctx // 2, ctx % 2
    y, z = ch // RING, ch % RING

    def up(a, by):
        return lax.rem(a + by + RING, RING)

    def on_x(by):
        return (up(x, by) * 2 + core, ch)

    def on_y(by):
        return (ctx, up(y, by) * RING + z)

    def on_z(by):
        return (ctx, y * RING + up(z, by))

    partner = (x * 2 + 1 - core, ch)

    def remote(src, dst, send, recv, device):
        return pltpu.make_async_remote_copy(
            src_ref=src, dst_ref=dst, send_sem=send, recv_sem=recv, device_id=device, device_id_type=MESH
        )

    def z_of(b):
        return (2, 1, -1, 0)[b]

    def w_cols(y_at, b):
        start = (y_at * RING + up(z, z_of(b))) * chan
        return pl.ds(pl.multiple_of(start, chan), chan)

    def eighth(x_at):
        return pl.multiple_of((core * RING + x_at) * slice_rows, slice_rows)

    def local_w(b):
        return pltpu.make_async_copy(w_ref.at[:, w_cols(y, b)], wblk.at[b, 0], lw_sem.at[b])

    def y_copy(b, j):
        at = pl.ds(eighth(x), slice_rows)
        return remote(
            w_ref.at[at, w_cols(up(y, -j), b)], wblk.at[b, j, at], y_s.at[b, j - 1], y_r.at[b, j - 1], on_y(-j)
        )

    def x_copy(b, kind):
        if kind < 2:
            at = pl.ds(eighth(x), slice_rows)
        elif kind == 2:
            at = pl.ds(eighth(up(x, -1)), slice_rows // 2)
        else:
            at = pl.ds(eighth(up(x, 1)) + slice_rows // 2, slice_rows // 2)
        ref = wblk.at[b, pl.ds(1, RING - 1), at]
        return remote(ref, ref, x_s.at[b, kind], x_r.at[b, kind], on_x(1 if kind % 2 == 0 else -1))

    def c_copy(b):
        ref = wblk.at[b, pl.ds(1, RING - 1), pl.ds(eighth(0), RING * slice_rows)]
        return remote(ref, ref, c_s.at[b], c_r.at[b], partner)

    def e_copy(grp, o):
        ref = ends.at[grp, ctx]
        return remote(ref, ref, e_s.at[grp, o - 1], e_r.at[grp, o - 1], (lax.rem(ctx + o, n_ctx), ch))

    def g_copy(c, kind):
        if kind < 2:
            src = gbuf.at[c, 0]
            dst = gbuf.at[c, 3 if kind == 0 else 1]
        elif kind == 2:
            src = gbuf.at[c, 3, pl.ds(0, half)]
            dst = gbuf.at[c, 2, pl.ds(0, half)]
        else:
            src = gbuf.at[c, 1, pl.ds(half, half)]
            dst = gbuf.at[c, 2, pl.ds(half, half)]
        return remote(src, dst, g_s.at[c, kind], g_r.at[c, kind], on_y(1 if kind % 2 == 0 else -1))

    def z_copy(c, kind):
        if kind < 2:
            src = s2.at[c, pl.ds(kind * half, half)]
            dst = r2.at[c, pl.ds(kind * half, half)]
        else:
            src = s1.at[c, kind - 2]
            dst = r1.at[c, kind - 2]
        return remote(src, dst, z_s.at[c, kind], z_r.at[c, kind], on_z(1 if kind % 2 == 0 else -1))

    small = [(res_hbm, res_ref), (rate_hbm, rate_ref), (skip_hbm, skip_ref), (q_hbm, q_ref)]
    small = [pltpu.make_async_copy(src, dst, in_sem.at[i]) for i, (src, dst) in enumerate(small)]

    def kv_copy(grp, which):
        lanes = pl.ds(pl.multiple_of(grp * LANES, LANES), LANES)
        src, dst = ((k_hbm, k_ref), (v_hbm, v_ref))[which]
        return pltpu.make_async_copy(src.at[:, lanes], dst.at[:, lanes], kv_sem.at[grp, which])

    small[0].start()
    small[1].start()
    small[2].start()
    for grp in range(groups):
        kv_copy(grp, 0).start()
        kv_copy(grp, 1).start()
    small[3].start()
    for b in range(RING):
        local_w(b).start()

    barrier = pltpu.get_barrier_semaphore()
    others = [(lax.rem(ctx + o, n_ctx), ch) for o in range(1, n_ctx)]
    others += [on_y(o) for o in range(1, RING)] + [on_z(1), on_z(-1)]
    for device in others:
        pl.semaphore_signal(barrier, inc=1, device_id=device, device_id_type=MESH)
    pl.semaphore_wait(barrier, len(others))

    def w_y_start(b):
        for j in (1, 3, 2):
            y_copy(b, j).start()

    def w_y_arrived(b):
        for j in range(1, RING):
            y_copy(b, j).wait_recv()

    def x_start(b):
        x_copy(b, 0).start()
        x_copy(b, 1).start()

    def w_x_arrived(b):
        x_copy(b, 0).wait_recv()
        x_copy(b, 2).start()
        x_copy(b, 1).wait_recv()
        x_copy(b, 3).start()

    def w_x_complete(b):
        x_copy(b, 2).wait_recv()
        x_copy(b, 3).wait_recv()
        c_copy(b).start()

    def w_complete(b):
        c_copy(b).wait_recv()
        local_w(b).wait()

    for b in range(RING - 1):
        w_y_start(b)
    small[0].wait()
    small[1].wait()
    small[2].wait()

    @pl.loop(0, groups)
    def _(grp):
        lanes = pl.ds(pl.multiple_of(grp * LANES, LANES), LANES)
        kv_copy(grp, 0).wait()
        kv_copy(grp, 1).wait()

        @pl.loop(0, tok // 64)
        def _(i):
            at = pl.ds(pl.multiple_of(i * 64, 64), 64)
            both = k_ref[at, lanes].astype(jnp.float32) * v_ref[at, lanes].astype(jnp.float32)
            gat[grp, at, :] = both.astype(jnp.bfloat16).astype(jnp.float32)

        rate = rate_ref[:, lanes]
        decay = jnp.exp(-rate)
        d = [jnp.broadcast_to(decay[m : m + 1], (SEGS, LANES)) for m in range(poles)]

        def step(j, s):
            g = gat[grp, pl.ds(j, SEGS, stride=seg_len), :]
            return tuple(s[m] * d[m] + g for m in range(poles))

        zero = jnp.zeros((SEGS, LANES), jnp.float32)
        s = lax.fori_loop(0, seg_len, step, (zero,) * poles, unroll=8)
        seg = lax.broadcasted_iota(jnp.int32, (SEGS, LANES), 0)
        ratio = [jnp.exp(-rate * float(seg_len * by)) for by in (1, 2, 4)]
        last = []
        for m in range(poles):
            run = s[m]
            for i, by in enumerate((1, 2, 4)):
                run = run + jnp.where(seg >= by, pltpu.roll(run, by, 0) * ratio[i][m : m + 1], 0.0)
            st[m, :, lanes] = run
            last.append(run[SEGS - 1 :])
        ends[grp, ctx] = jnp.concatenate(last, axis=0)
        for o in range(1, n_ctx):
            e_copy(grp, o).start()

    w_y_arrived(0)
    x_start(0)
    small[3].wait()

    @pl.loop(0, groups)
    def _(grp):
        @pl.when(grp == groups - 1)
        def _():
            w_y_arrived(1)
            x_start(1)

        lanes = pl.ds(pl.multiple_of(grp * LANES, LANES), LANES)
        for o in range(1, n_ctx):
            e_copy(grp, o).wait_recv()
        rate = rate_ref[:, lanes]
        whole = jnp.exp(-rate * float(tok))
        state_in = jnp.zeros((poles, LANES), jnp.float32)
        for o in range(n_ctx - 1):
            state_in = jnp.where(o < ctx, state_in * whole + ends[grp, o], state_in)
        seg = lax.broadcasted_iota(jnp.int32, (SEGS, LANES), 0)
        behind = seg.astype(jnp.float32) * float(seg_len)
        for m in range(poles):
            before = jnp.where(seg >= 1, pltpu.roll(st[m, :, lanes], 1, 0), 0.0)
            st[m, :, lanes] = before + jnp.exp(-rate[m : m + 1] * behind) * state_in[m : m + 1]

    def second_pass(c):
        @pl.loop(0, groups)
        def _(grp):
            lanes = pl.ds(pl.multiple_of(grp * LANES, LANES), LANES)
            decay = jnp.exp(-rate_ref[:, lanes])
            d = [jnp.broadcast_to(decay[m : m + 1], (SEGS, LANES)) for m in range(poles)]
            weight = res_ref[:, lanes]
            w = [jnp.broadcast_to(weight[m : m + 1], (SEGS, LANES)) for m in range(poles)]
            skip = jnp.broadcast_to(skip_ref[:, lanes], (SEGS, LANES))

            def step(j, s):
                g = gat[grp, pl.ds(c * steps + j, SEGS, stride=seg_len), :]
                s = tuple(s[m] * d[m] + g for m in range(poles))
                parts = [s[m] * w[m] for m in range(poles)]
                while len(parts) > 1:
                    parts = [a + b for a, b in zip(parts[::2], parts[1::2])]
                mixed[grp, pl.ds(j, SEGS, stride=steps), :] = parts[0] + skip * g
                return s

            s = lax.fori_loop(0, steps, step, tuple(st[m, :, lanes] for m in range(poles)), unroll=8)
            for m in range(poles):
                st[m, :, lanes] = s[m]

        @pl.loop(0, SEGS)
        def _(i):
            at = pl.ds(pl.multiple_of(i * steps, steps), steps)
            q = q_ref[pl.ds(pl.multiple_of(i * seg_len + c * steps, steps), steps), :]
            for grp in range(groups):
                lanes = slice(grp * LANES, (grp + 1) * LANES)
                gbuf[c, 0, at, lanes] = (q[:, lanes].astype(jnp.float32) * mixed[grp, at, :]).astype(jnp.bfloat16)

    def g_start(c):
        g_copy(c, 0).start()
        g_copy(c, 1).start()

    def g_arrived(c):
        g_copy(c, 0).wait_recv()
        g_copy(c, 2).start()
        g_copy(c, 1).wait_recv()
        g_copy(c, 3).start()

    def product(c, b):
        total = None
        for j in range(RING):
            part = jnp.dot(gbuf[c, j], wblk[b, j], preferred_element_type=jnp.float32)
            total = part if total is None else total + part
        return total

    @pl.loop(0, CHUNKS)
    def _(c):
        second_pass(c)

        @pl.when(c < 2)
        def _():
            g_start(c)

        @pl.when(c == 1)
        def _():
            w_y_start(3)
            w_x_arrived(0)
            w_y_arrived(2)
            x_start(2)

        @pl.when(c == 5)
        def _():
            w_x_arrived(1)
            g_arrived(0)
            g_start(2)

        @pl.when(c == 6)
        def _():
            w_x_complete(0)

        @pl.when(c == 7)
        def _():
            g_arrived(1)
            g_start(3)

    def block_0(c):
        g_copy(c, 2).wait_recv()
        g_copy(c, 3).wait_recv()
        s2[c] = product(c, 0).astype(jnp.bfloat16)
        z_copy(c, 0).start()
        z_copy(c, 1).start()

    def block_1(c):
        total = product(c, 1)
        z_copy(c, 0).wait_recv()
        s1[c, 0, pl.ds(0, half), :] = (total[:half] + r2[c, pl.ds(0, half), :].astype(jnp.float32)).astype(jnp.bfloat16)
        s1[c, 0, pl.ds(half, half), :] = total[half:].astype(jnp.bfloat16)
        z_copy(c, 2).start()

    def block_2(c):
        total = product(c, 2)
        z_copy(c, 1).wait_recv()
        s1[c, 1, pl.ds(0, half), :] = total[:half].astype(jnp.bfloat16)
        s1[c, 1, pl.ds(half, half), :] = (total[half:] + r2[c, pl.ds(half, half), :].astype(jnp.float32)).astype(jnp.bfloat16)
        z_copy(c, 3).start()

    def block_3(c):
        total = product(c, 3)
        z_copy(c, 2).wait_recv()
        z_copy(c, 3).wait_recv()
        total = (total + r1[c, 0].astype(jnp.float32) + r1[c, 1].astype(jnp.float32)).astype(jnp.bfloat16)
        out_buf[c] = total
        for seg in range(SEGS):
            out_copy(c, seg).start()

    def out_copy(c, seg):
        return pltpu.make_async_copy(
            out_buf.at[c, pl.ds(seg * steps, steps)],
            out_ref.at[pl.ds(pl.multiple_of(seg * seg_len + c * steps, steps), steps)],
            out_sem.at[c, seg],
        )

    w_complete(0)

    @pl.loop(0, CHUNKS + 1)
    def _(i):
        @pl.when(i < CHUNKS)
        def _():
            block_0(i)

        @pl.when(i == 0)
        def _():
            w_x_arrived(2)
            w_y_arrived(3)
            x_start(3)

        @pl.when(i + 2 < CHUNKS)
        def _():
            g_arrived(i + 2)

        @pl.when(i + 4 < CHUNKS)
        def _():
            g_start(i + 4)

        @pl.when(i == 0)
        def _():
            w_x_complete(1)

        @pl.when(i == 1)
        def _():
            w_complete(1)
            w_x_complete(2)

        @pl.when(i >= 1)
        def _():
            block_1(i - 1)

        @pl.when(i == 1)
        def _():
            w_complete(2)

        @pl.when(i >= 1)
        def _():
            block_2(i - 1)

        @pl.when(i == 2)
        def _():
            w_x_arrived(3)

        @pl.when(i == 3)
        def _():
            w_x_complete(3)

        @pl.when(i == 5)
        def _():
            w_complete(3)

        @pl.when(i >= 5)
        def _():
            block_3(i - 5)

    @pl.loop(CHUNKS - 4, CHUNKS)
    def _(c):
        block_3(c)

    for grp in range(groups):
        for o in range(1, n_ctx):
            e_copy(grp, o).wait_send()
    for b in range(RING):
        for j in range(1, RING):
            y_copy(b, j).wait_send()
        for kind in range(4):
            x_copy(b, kind).wait_send()
        c_copy(b).wait_send()

    @pl.loop(0, CHUNKS)
    def _(c):
        for kind in range(4):
            g_copy(c, kind).wait_send()
            z_copy(c, kind).wait_send()
        for seg in range(SEGS):
            out_copy(c, seg).wait()


def shards(query_branch, key_branch, value_branch, residue, decay_rate, skip_gain, out_weight):
    tok, chan = key_branch.shape
    poles = residue.shape[0]
    rows = tok // CHUNKS
    n_ctx = 2 * RING
    dma = pltpu.SemaphoreType.DMA
    bf16, f32 = jnp.bfloat16, jnp.float32
    return pl.pallas_call(
        kernel,
        out_shape=jax.ShapeDtypeStruct((tok, chan), bf16),
        in_specs=[pl.BlockSpec(memory_space=pltpu.HBM)] * 7,
        out_specs=pl.BlockSpec(memory_space=pl.ANY),
        scratch_shapes=[
            pltpu.VMEM((tok, chan), bf16),
            pltpu.VMEM((tok, chan), bf16),
            pltpu.VMEM((tok, chan), bf16),
            pltpu.VMEM((poles, chan), f32),
            pltpu.VMEM((poles, chan), f32),
            pltpu.VMEM((1, chan), f32),
            pltpu.VMEM((CHUNKS, rows, chan), bf16),
            pltpu.VMEM((chan // LANES, tok, LANES), f32),
            pltpu.VMEM((poles, SEGS, chan), f32),
            pltpu.VMEM((chan // LANES, n_ctx, poles, LANES), f32),
            pltpu.VMEM((chan // LANES, rows, LANES), f32),
            pltpu.VMEM((RING, RING, chan, chan), bf16),
            pltpu.VMEM((CHUNKS, RING, rows, chan), bf16),
            pltpu.VMEM((CHUNKS, rows, chan), bf16),
            pltpu.VMEM((CHUNKS, rows, chan), bf16),
            pltpu.VMEM((CHUNKS, 2, rows, chan), bf16),
            pltpu.VMEM((CHUNKS, 2, rows, chan), bf16),
            dma((4,)), dma((chan // LANES, 2)), dma((CHUNKS, SEGS)), dma((RING,)),
            dma((RING, RING - 1)), dma((RING, RING - 1)),
            dma((RING, 4)), dma((RING, 4)),
            dma((RING,)), dma((RING,)),
            dma((chan // LANES, n_ctx - 1)), dma((chan // LANES, n_ctx - 1)),
            dma((CHUNKS, 4)), dma((CHUNKS, 4)),
            dma((CHUNKS, 4)), dma((CHUNKS, 4)),
        ],
        compiler_params=pltpu.CompilerParams(
            collective_id=0, has_side_effects=True, vmem_limit_bytes=63 * 1024 * 1024
        ),
        cost_estimate=pl.CostEstimate(
            flops=2 * tok * chan * chan * 16, bytes_accessed=12 * 1024 * 1024, transcendentals=0
        ),
    )(query_branch, key_branch, value_branch, residue, decay_rate, skip_gain.reshape(1, chan), out_weight)


def solution(mesh):
    in_specs = (
        P("ctx", "ch"),
        P("ctx", "ch"),
        P("ctx", "ch"),
        P(None, "ch"),
        P(None, "ch"),
        P("ch"),
        P("ch", None),
    )
    return jax.shard_map(shards, mesh=mesh, in_specs=in_specs, out_specs=P("ctx", "ch"), check_vma=False)
```

```python
import functools

import jax
import jax.numpy as jnp
from jax import lax
from jax.experimental import pallas as pl
from jax.experimental.pallas import tpu as pltpu
from jax.sharding import PartitionSpec as P

MESH = pl.DeviceIdType.MESH
SEGS = 8
CHUNKS = 8
RING = 4
LANES = 128


def kernel(
    q_hbm, k_hbm, v_hbm, res_hbm, rate_hbm, skip_hbm, w_ref, out_ref,
    q_ref, k_ref, v_ref, res_ref, rate_ref, skip_ref, out_buf,
    gat, st, ends, mixed, wblk, gbuf, s2, r2, s1, r1,
    in_sem, kv_sem, out_sem, lw_sem, y_s, y_r, x_s, x_r, c_s, c_r, e_s, e_r, g_s, g_r, z_s, z_r,
):
    tok, chan = k_ref.shape
    poles = res_ref.shape[0]
    seg_len = tok // SEGS
    steps = seg_len // CHUNKS
    rows = SEGS * steps
    half = rows // 2
    groups = chan // LANES
    n_ctx = 2 * RING
    slice_rows = chan // n_ctx

    ctx = lax.axis_index("ctx")
    ch = lax.axis_index("ch")
    x, core = ctx // 2, ctx % 2
    y, z = ch // RING, ch % RING

    def up(a, by):
        return lax.rem(a + by + RING, RING)

    def on_x(by):
        return (up(x, by) * 2 + core, ch)

    def on_y(by):
        return (ctx, up(y, by) * RING + z)

    def on_z(by):
        return (ctx, y * RING + up(z, by))

    partner = (x * 2 + 1 - core, ch)

    def remote(src, dst, send, recv, device):
        return pltpu.make_async_remote_copy(
            src_ref=src, dst_ref=dst, send_sem=send, recv_sem=recv, device_id=device, device_id_type=MESH
        )

    def z_of(b):
        return (2, 1, -1, 0)[b]

    def w_cols(y_at, b):
        start = (y_at * RING + up(z, z_of(b))) * chan
        return pl.ds(pl.multiple_of(start, chan), chan)

    def eighth(x_at):
        return pl.multiple_of((core * RING + x_at) * slice_rows, slice_rows)

    def local_w(b):
        return pltpu.make_async_copy(w_ref.at[:, w_cols(y, b)], wblk.at[b, 0], lw_sem.at[b])

    def y_copy(b, j):
        at = pl.ds(eighth(x), slice_rows)
        return remote(
            w_ref.at[at, w_cols(up(y, -j), b)], wblk.at[b, j, at], y_s.at[b, j - 1], y_r.at[b, j - 1], on_y(-j)
        )

    def x_copy(b, kind):
        if kind < 2:
            at = pl.ds(eighth(x), slice_rows)
        elif kind == 2:
            at = pl.ds(eighth(up(x, -1)), slice_rows // 2)
        else:
            at = pl.ds(eighth(up(x, 1)) + slice_rows // 2, slice_rows // 2)
        ref = wblk.at[b, pl.ds(1, RING - 1), at]
        return remote(ref, ref, x_s.at[b, kind], x_r.at[b, kind], on_x(1 if kind % 2 == 0 else -1))

    def c_copy(b):
        ref = wblk.at[b, pl.ds(1, RING - 1), pl.ds(eighth(0), RING * slice_rows)]
        return remote(ref, ref, c_s.at[b], c_r.at[b], partner)

    def e_copy(grp, o):
        ref = ends.at[grp, ctx]
        return remote(ref, ref, e_s.at[grp, o - 1], e_r.at[grp, o - 1], (lax.rem(ctx + o, n_ctx), ch))

    def g_copy(c, kind):
        if kind < 2:
            src = gbuf.at[c, 0]
            dst = gbuf.at[c, 3 if kind == 0 else 1]
        elif kind == 2:
            src = gbuf.at[c, 3, pl.ds(0, half)]
            dst = gbuf.at[c, 2, pl.ds(0, half)]
        else:
            src = gbuf.at[c, 1, pl.ds(half, half)]
            dst = gbuf.at[c, 2, pl.ds(half, half)]
        return remote(src, dst, g_s.at[c, kind], g_r.at[c, kind], on_y(1 if kind % 2 == 0 else -1))

    def z_copy(c, kind):
        if kind < 2:
            src = s2.at[c, pl.ds(kind * half, half)]
            dst = r2.at[c, pl.ds(kind * half, half)]
        else:
            src = s1.at[c, kind - 2]
            dst = r1.at[c, kind - 2]
        return remote(src, dst, z_s.at[c, kind], z_r.at[c, kind], on_z(1 if kind % 2 == 0 else -1))

    small = [(res_hbm, res_ref), (rate_hbm, rate_ref), (skip_hbm, skip_ref), (q_hbm, q_ref)]
    small = [pltpu.make_async_copy(src, dst, in_sem.at[i]) for i, (src, dst) in enumerate(small)]

    def kv_copy(grp, which):
        lanes = pl.ds(pl.multiple_of(grp * LANES, LANES), LANES)
        src, dst = ((k_hbm, k_ref), (v_hbm, v_ref))[which]
        return pltpu.make_async_copy(src.at[:, lanes], dst.at[:, lanes], kv_sem.at[grp, which])

    barrier = pltpu.get_barrier_semaphore()
    others = [(lax.rem(ctx + o, n_ctx), ch) for o in range(1, n_ctx)]
    others += [on_y(o) for o in range(1, RING)] + [on_z(1), on_z(-1)]
    for device in others:
        pl.semaphore_signal(barrier, inc=1, device_id=device, device_id_type=MESH)

    small[0].start()
    small[1].start()
    small[2].start()
    for grp in range(groups):
        kv_copy(grp, 0).start()
        kv_copy(grp, 1).start()
    small[3].start()
    for b in range(RING):
        local_w(b).start()

    def w_y_start(b):
        for j in (1, 3, 2):
            y_copy(b, j).start()

    def w_y_arrived(b):
        for j in range(1, RING):
            y_copy(b, j).wait_recv()

    def x_start(b):
        x_copy(b, 0).start()
        x_copy(b, 1).start()

    def w_x_arrived(b):
        x_copy(b, 0).wait_recv()
        x_copy(b, 2).start()
        x_copy(b, 1).wait_recv()
        x_copy(b, 3).start()

    def w_x_complete(b):
        x_copy(b, 2).wait_recv()
        x_copy(b, 3).wait_recv()
        c_copy(b).start()

    def w_complete(b):
        c_copy(b).wait_recv()
        local_w(b).wait()

    small[0].wait()
    small[1].wait()
    small[2].wait()

    def first_pass(grp):
        lanes = pl.ds(pl.multiple_of(grp * LANES, LANES), LANES)
        kv_copy(grp, 0).wait()
        kv_copy(grp, 1).wait()

        @pl.loop(0, tok // 64)
        def _(i):
            at = pl.ds(pl.multiple_of(i * 64, 64), 64)
            both = k_ref[at, lanes].astype(jnp.float32) * v_ref[at, lanes].astype(jnp.float32)
            gat[grp, at, :] = both.astype(jnp.bfloat16).astype(jnp.float32)

        rate = rate_ref[:, lanes]
        decay = jnp.exp(-rate)
        d = [jnp.broadcast_to(decay[m : m + 1], (SEGS, LANES)) for m in range(poles)]

        def step(j, s):
            g = gat[grp, pl.ds(j, SEGS, stride=seg_len), :]
            return tuple(s[m] * d[m] + g for m in range(poles))

        zero = jnp.zeros((SEGS, LANES), jnp.float32)
        s = lax.fori_loop(0, seg_len, step, (zero,) * poles, unroll=8)
        seg = lax.broadcasted_iota(jnp.int32, (SEGS, LANES), 0)
        ratio = [jnp.exp(-rate * float(seg_len * by)) for by in (1, 2, 4)]
        last = []
        for m in range(poles):
            run = s[m]
            for i, by in enumerate((1, 2, 4)):
                run = run + jnp.where(seg >= by, pltpu.roll(run, by, 0) * ratio[i][m : m + 1], 0.0)
            st[m, :, lanes] = run
            last.append(run[SEGS - 1 :])
        ends[grp, ctx] = jnp.concatenate(last, axis=0)

    def ends_start(grp):
        for o in range(1, n_ctx):
            e_copy(grp, o).start()

    first_pass(0)
    pl.semaphore_wait(barrier, len(others))
    for b in range(RING - 1):
        w_y_start(b)
    ends_start(0)

    @pl.loop(1, groups)
    def _(grp):
        first_pass(grp)
        ends_start(grp)

    w_y_arrived(0)
    x_start(0)
    small[3].wait()

    @pl.loop(0, groups)
    def _(grp):
        @pl.when(grp == groups - 1)
        def _():
            w_y_arrived(1)
            x_start(1)

        lanes = pl.ds(pl.multiple_of(grp * LANES, LANES), LANES)
        for o in range(1, n_ctx):
            e_copy(grp, o).wait_recv()
        rate = rate_ref[:, lanes]
        whole = jnp.exp(-rate * float(tok))
        state_in = jnp.zeros((poles, LANES), jnp.float32)
        for o in range(n_ctx - 1):
            state_in = jnp.where(o < ctx, state_in * whole + ends[grp, o], state_in)
        seg = lax.broadcasted_iota(jnp.int32, (SEGS, LANES), 0)
        behind = seg.astype(jnp.float32) * float(seg_len)
        for m in range(poles):
            before = jnp.where(seg >= 1, pltpu.roll(st[m, :, lanes], 1, 0), 0.0)
            st[m, :, lanes] = before + jnp.exp(-rate[m : m + 1] * behind) * state_in[m : m + 1]

    def second_pass(c):
        @pl.loop(0, groups)
        def _(grp):
            lanes = pl.ds(pl.multiple_of(grp * LANES, LANES), LANES)
            decay = jnp.exp(-rate_ref[:, lanes])
            d = [jnp.broadcast_to(decay[m : m + 1], (SEGS, LANES)) for m in range(poles)]
            weight = res_ref[:, lanes]
            w = [jnp.broadcast_to(weight[m : m + 1], (SEGS, LANES)) for m in range(poles)]
            skip = jnp.broadcast_to(skip_ref[:, lanes], (SEGS, LANES))

            def step(j, s):
                g = gat[grp, pl.ds(c * steps + j, SEGS, stride=seg_len), :]
                s = tuple(s[m] * d[m] + g for m in range(poles))
                parts = [s[m] * w[m] for m in range(poles)]
                while len(parts) > 1:
                    parts = [a + b for a, b in zip(parts[::2], parts[1::2])]
                mixed[grp, pl.ds(j, SEGS, stride=steps), :] = parts[0] + skip * g
                return s

            s = lax.fori_loop(0, steps, step, tuple(st[m, :, lanes] for m in range(poles)), unroll=8)
            for m in range(poles):
                st[m, :, lanes] = s[m]

        @pl.loop(0, SEGS)
        def _(i):
            at = pl.ds(pl.multiple_of(i * steps, steps), steps)
            q = q_ref[pl.ds(pl.multiple_of(i * seg_len + c * steps, steps), steps), :]
            for grp in range(groups):
                lanes = slice(grp * LANES, (grp + 1) * LANES)
                gbuf[c, 0, at, lanes] = (q[:, lanes].astype(jnp.float32) * mixed[grp, at, :]).astype(jnp.bfloat16)

    def g_start(c):
        g_copy(c, 0).start()
        g_copy(c, 1).start()

    def g_arrived(c):
        g_copy(c, 0).wait_recv()
        g_copy(c, 2).start()
        g_copy(c, 1).wait_recv()
        g_copy(c, 3).start()

    def product(c, b):
        total = None
        for j in range(RING):
            part = jnp.dot(gbuf[c, j], wblk[b, j], preferred_element_type=jnp.float32)
            total = part if total is None else total + part
        return total

    @pl.loop(0, CHUNKS)
    def _(c):
        second_pass(c)

        @pl.when(c < 2)
        def _():
            g_start(c)

        @pl.when(c == 1)
        def _():
            w_y_start(3)
            w_x_arrived(0)
            w_y_arrived(2)
            x_start(2)

        @pl.when(c == 5)
        def _():
            w_x_arrived(1)
            g_arrived(0)
            g_start(2)

        @pl.when(c == 6)
        def _():
            w_x_complete(0)

        @pl.when(c == 7)
        def _():
            g_arrived(1)
            g_start(3)

    def block_0(c):
        g_copy(c, 2).wait_recv()
        g_copy(c, 3).wait_recv()
        s2[c] = product(c, 0).astype(jnp.bfloat16)
        z_copy(c, 0).start()
        z_copy(c, 1).start()

    def block_1(c):
        total = product(c, 1)
        z_copy(c, 0).wait_recv()
        s1[c, 0, pl.ds(0, half), :] = (total[:half] + r2[c, pl.ds(0, half), :].astype(jnp.float32)).astype(jnp.bfloat16)
        s1[c, 0, pl.ds(half, half), :] = total[half:].astype(jnp.bfloat16)
        z_copy(c, 2).start()

    def block_2(c):
        total = product(c, 2)
        z_copy(c, 1).wait_recv()
        s1[c, 1, pl.ds(0, half), :] = total[:half].astype(jnp.bfloat16)
        s1[c, 1, pl.ds(half, half), :] = (total[half:] + r2[c, pl.ds(half, half), :].astype(jnp.float32)).astype(jnp.bfloat16)
        z_copy(c, 3).start()

    def block_3(c):
        total = product(c, 3)
        z_copy(c, 2).wait_recv()
        z_copy(c, 3).wait_recv()
        total = (total + r1[c, 0].astype(jnp.float32) + r1[c, 1].astype(jnp.float32)).astype(jnp.bfloat16)
        out_buf[c] = total
        for seg in range(SEGS):
            out_copy(c, seg).start()

    def out_copy(c, seg):
        return pltpu.make_async_copy(
            out_buf.at[c, pl.ds(seg * steps, steps)],
            out_ref.at[pl.ds(pl.multiple_of(seg * seg_len + c * steps, steps), steps)],
            out_sem.at[c, seg],
        )

    w_complete(0)

    @pl.loop(0, CHUNKS + 1)
    def _(i):
        @pl.when(i < CHUNKS)
        def _():
            block_0(i)

        @pl.when(i == 0)
        def _():
            w_x_arrived(2)
            w_y_arrived(3)
            x_start(3)

        @pl.when(i + 2 < CHUNKS)
        def _():
            g_arrived(i + 2)

        @pl.when(i + 4 < CHUNKS)
        def _():
            g_start(i + 4)

        @pl.when(i == 0)
        def _():
            w_x_complete(1)

        @pl.when(i == 1)
        def _():
            w_complete(1)
            w_x_complete(2)

        @pl.when(i >= 1)
        def _():
            block_1(i - 1)

        @pl.when(i == 1)
        def _():
            w_complete(2)

        @pl.when(i >= 1)
        def _():
            block_2(i - 1)

        @pl.when(i == 2)
        def _():
            w_x_arrived(3)

        @pl.when(i == 3)
        def _():
            w_x_complete(3)

        @pl.when(i == 5)
        def _():
            w_complete(3)

        @pl.when(i >= 5)
        def _():
            block_3(i - 5)

    @pl.loop(CHUNKS - 4, CHUNKS)
    def _(c):
        block_3(c)

    for grp in range(groups):
        for o in range(1, n_ctx):
            e_copy(grp, o).wait_send()
    for b in range(RING):
        for j in range(1, RING):
            y_copy(b, j).wait_send()
        for kind in range(4):
            x_copy(b, kind).wait_send()
        c_copy(b).wait_send()

    @pl.loop(0, CHUNKS)
    def _(c):
        for kind in range(4):
            g_copy(c, kind).wait_send()
            z_copy(c, kind).wait_send()
        for seg in range(SEGS):
            out_copy(c, seg).wait()


def shards(query_branch, key_branch, value_branch, residue, decay_rate, skip_gain, out_weight):
    tok, chan = key_branch.shape
    poles = residue.shape[0]
    rows = tok // CHUNKS
    n_ctx = 2 * RING
    dma = pltpu.SemaphoreType.DMA
    bf16, f32 = jnp.bfloat16, jnp.float32
    return pl.pallas_call(
        kernel,
        out_shape=jax.ShapeDtypeStruct((tok, chan), bf16),
        in_specs=[pl.BlockSpec(memory_space=pltpu.HBM)] * 7,
        out_specs=pl.BlockSpec(memory_space=pl.ANY),
        scratch_shapes=[
            pltpu.VMEM((tok, chan), bf16),
            pltpu.VMEM((tok, chan), bf16),
            pltpu.VMEM((tok, chan), bf16),
            pltpu.VMEM((poles, chan), f32),
            pltpu.VMEM((poles, chan), f32),
            pltpu.VMEM((1, chan), f32),
            pltpu.VMEM((CHUNKS, rows, chan), bf16),
            pltpu.VMEM((chan // LANES, tok, LANES), f32),
            pltpu.VMEM((poles, SEGS, chan), f32),
            pltpu.VMEM((chan // LANES, n_ctx, poles, LANES), f32),
            pltpu.VMEM((chan // LANES, rows, LANES), f32),
            pltpu.VMEM((RING, RING, chan, chan), bf16),
            pltpu.VMEM((CHUNKS, RING, rows, chan), bf16),
            pltpu.VMEM((CHUNKS, rows, chan), bf16),
            pltpu.VMEM((CHUNKS, rows, chan), bf16),
            pltpu.VMEM((CHUNKS, 2, rows, chan), bf16),
            pltpu.VMEM((CHUNKS, 2, rows, chan), bf16),
            dma((4,)), dma((chan // LANES, 2)), dma((CHUNKS, SEGS)), dma((RING,)),
            dma((RING, RING - 1)), dma((RING, RING - 1)),
            dma((RING, 4)), dma((RING, 4)),
            dma((RING,)), dma((RING,)),
            dma((chan // LANES, n_ctx - 1)), dma((chan // LANES, n_ctx - 1)),
            dma((CHUNKS, 4)), dma((CHUNKS, 4)),
            dma((CHUNKS, 4)), dma((CHUNKS, 4)),
        ],
        compiler_params=pltpu.CompilerParams(
            collective_id=0, has_side_effects=True, vmem_limit_bytes=63 * 1024 * 1024
        ),
        cost_estimate=pl.CostEstimate(
            flops=2 * tok * chan * chan * 16, bytes_accessed=12 * 1024 * 1024, transcendentals=0
        ),
    )(query_branch, key_branch, value_branch, residue, decay_rate, skip_gain.reshape(1, chan), out_weight)


def solution(mesh):
    in_specs = (
        P("ctx", "ch"),
        P("ctx", "ch"),
        P("ctx", "ch"),
        P(None, "ch"),
        P(None, "ch"),
        P("ch"),
        P("ch", None),
    )
    return jax.shard_map(shards, mesh=mesh, in_specs=in_specs, out_specs=P("ctx", "ch"), check_vma=False)
```
